32 devices in a mesh: px: 8 (over y, x, core), py: 4 (over z).
Axes of the slice: x: 2, y: 2, z: 4, core: 2. Of those that a mesh axis runs over, the one named last changes fastest.
Arguments:
- base_flow: float32 [768, 384, 768], P('px', 'py'), may hold values from -6 to 6
- tangent: float32 [768, 384, 768], P('px', 'py'), may hold values from -6 to 6
- kx_bounds: int32 [2, 320], replicated, may hold values from 0 to 320, as said below
- left_basis: float32 [384, 384], replicated, may hold values from -0.3125 to 0.3125
- right_basis: float32 [384, 384], replicated, may hold values from -0.3125 to 0.3125
- eigenvalues: float32 [384], replicated, may hold values from 0.05 to 20
- wall_rows: float32 [2, 384], replicated, may hold values from -0.3125 to 0.3125
- sources: float32 [2, 384], replicated, may hold values from -6 to 6
- influence: float32 [4, 320, 320], P(None, 'py', 'px'), may hold values from -6 to 6
Outputs:
- response: float32 [384, 320, 2, 320], P(None, 'py', None, 'px')
The draws below stay inside these ranges and needn't reach their ends.
Inputs may be any that keep to these rules, and one draw needn't show every extreme that they name: kx_bounds[0, b] is at most 80 and kx_bounds[1, b] at least 240; the first column keeps every streamwise wavenumber.
All inputs are finite; a program needn't handle non-finite values.
Results may differ from the reference program's by a relative error of at most 0.000078.
Values sent between devices are 32-bit elements; how exact they have to be, the bound alone decides.
A program may use at most 192 MiB of HBM per device.

```python
import math
import jax
import jax.numpy as jnp
from jax import lax

NX = 768
NY = 384
NZ = 768
MX = 160
MZ = 160
KX = 320
KZ = 320


def draw_kx_bounds(key, part):
    key = jax.random.fold_in(key, 11)
    first_key, second_key = jax.random.split(key)
    lower_edge = jax.random.randint(first_key, (KZ,), 0, MX // 2 + 1)
    upper_edge = jax.random.randint(second_key, (KZ,), KX - MX // 2, KX + 1)
    lower_edge = lower_edge.at[0].set(0)
    upper_edge = upper_edge.at[0].set(KX)
    return jnp.stack([lower_edge, upper_edge]).astype(jnp.int32)


def levels(own_key, dims, pieces, low, top_value):
    level = 1.0
    for dim, blocks in pieces:
        steps = jax.random.uniform(jax.random.fold_in(jax.random.fold_in(own_key, 6), dim), (blocks,), jnp.float32, low / len(pieces), top_value / len(pieces))
        level = level * jnp.repeat(jnp.exp(steps), dims[dim] // blocks).reshape((-1,) + (1,) * (len(dims) - 1 - dim))
    return level


def bell_draw(rng, dims, width, reach, cuts=(), held_as=jnp.bfloat16):
    drawn = width * jax.random.normal(rng, dims, jnp.float32)
    if cuts:
        drawn = drawn * levels(rng, dims, cuts, -0.22, 0.18)
    return jnp.clip(drawn, -reach, reach).astype(held_as)


def setup_inputs(seed: int = 0) -> dict:
    splits = jax.random.split(jax.random.key(seed), 10)
    return {
        "base_flow": bell_draw(splits[0], (NX, NY, NZ), 1.0, 6.0, ((0, 8), (1, 4)), jnp.float32),
        "tangent": bell_draw(splits[1], (NX, NY, NZ), 1.0, 6.0, ((0, 8), (1, 4)), jnp.float32),
        "kx_bounds": draw_kx_bounds(jax.random.fold_in(splits[9], 71), 0),
        "left_basis": bell_draw(splits[3], (NY, NY), NY ** -0.5, 0.3125, (), jnp.float32),
        "right_basis": bell_draw(splits[4], (NY, NY), NY ** -0.5, 0.3125, (), jnp.float32),
        "eigenvalues": jnp.clip(jnp.exp(jax.random.uniform(splits[5], (NY,), jnp.float32, math.log(0.05), math.log(20.0))), 0.05, 20.0),
        "wall_rows": bell_draw(splits[6], (2, NY), NY ** -0.5, 0.3125, (), jnp.float32),
        "sources": bell_draw(splits[7], (2, NY), 1.0, 6.0, (), jnp.float32),
        "influence": bell_draw(splits[8], (4, KX, KZ), 1.0, 6.0, ((1, 4), (2, 8)), jnp.float32),
    }


def reference(base_flow, tangent, kx_bounds, left_basis, right_basis, eigenvalues, wall_rows, sources, influence):
    kx_index = (jnp.arange(KX) - MX) % NX
    kz_index = (jnp.arange(KZ) - MZ) % NZ

    def y_plane(level):
        product = base_flow[:, level, :] * tangent[:, level, :]
        plane_modes = jnp.fft.fft2(product) / math.sqrt(NX * NZ)
        plane_modes = plane_modes[kx_index][:, kz_index]
        return jnp.stack([jnp.real(plane_modes), jnp.imag(plane_modes)]).astype(product.dtype)
    modes = lax.map(y_plane, jnp.arange(NY))
    modes = jnp.transpose(modes, (1, 2, 3, 0))
    kx_scaled = (jnp.arange(KX) - MX).astype(jnp.float32) / MX
    kz_scaled = (jnp.arange(KZ) - MZ).astype(jnp.float32) / MZ
    factor = kx_scaled[:, None, None]
    forcing = jnp.stack([-factor * modes[1], factor * modes[0]])
    columns = jnp.arange(KX)
    keep_mask = (columns[:, None] >= kx_bounds[0][None, :]) & (columns[:, None] < kx_bounds[1][None, :])
    forcing = jnp.where(keep_mask[None, :, :, None], forcing, jnp.zeros_like(forcing))
    shift = kx_scaled[:, None] ** 2 + kz_scaled[None, :] ** 2
    mode_gain = 1.0 / (1.0 + eigenvalues[None, None, :] + shift[:, :, None])
    highest = lax.Precision.HIGHEST
    projected = jnp.einsum('cabj,ij->cabi', forcing, left_basis, precision=highest)
    particular = jnp.einsum('cabj,ij->cabi', mode_gain[None] * projected, right_basis, precision=highest)
    source_proj = jnp.einsum('sj,ij->si', sources, left_basis, precision=highest)
    homogeneous = jnp.einsum('sabj,ij->sabi', mode_gain[None] * source_proj[:, None, None, :], right_basis, precision=highest)
    wall_values = jnp.einsum('cabi,wi->cabw', particular, wall_rows, precision=highest)
    inverse_map = influence.reshape(2, 2, KX, KZ)
    coefficients = -jnp.einsum('swab,cabw->cabs', inverse_map, wall_values, precision=highest)
    result = particular + jnp.einsum('cabs,sabi->cabi', coefficients, homogeneous, precision=highest)
    return jnp.transpose(result, (3, 1, 0, 2))
```

```python
import math

import jax
import jax.numpy as jnp
from jax import lax
from jax.experimental import pallas as pl
from jax.experimental.pallas import tpu as pltpu
from jax.sharding import PartitionSpec as P

HIGH = lax.Precision.HIGH
PARTS = 3
LANES = 128
CHUNKS = 5
VMEM_BYTES = 48 * 1024 * 1024


def dft_tables(length, kept):
    points = jnp.arange(length, dtype=jnp.int32)
    waves = jnp.arange(kept, dtype=jnp.int32) - kept // 2
    turns = waves[:, None] * points[None, :] % length
    angles = turns.astype(jnp.float32) * (2.0 * math.pi / length)
    scale_factor = 1.0 / math.sqrt(length)
    return (jnp.cos(angles) * scale_factor, jnp.sin(angles) * scale_factor)


def make_body(px_size, py_size):
    def body(
        base_flow,
        tangent,
        kx_bounds,
        left_basis,
        right_basis,
        eigenvalues,
        wall_rows,
        sources,
        influence,
    ):
        x_count, y_count, nz = base_flow.shape
        nx = x_count * px_size
        ny = y_count * py_size
        kz_local = influence.shape[2]
        kx_local = influence.shape[1]
        kz_all = kz_local * px_size
        kx_all = kx_local * py_size
        mx = kx_all // 2
        mz = kz_all // 2
        parts = PARTS if (kz_local * (y_count // PARTS)) % 128 == 0 else 1
        rows = y_count // parts

        z_cosine, z_sine = dft_tables(nz, kz_all)
        z_table = jnp.stack(
            [z_cosine.reshape(px_size, kz_local, nz), -z_sine.reshape(px_size, kz_local, nz)],
            axis=1,
        ).reshape(px_size * 2 * kz_local, nz)

        kx_scaled = (jnp.arange(kx_all, dtype=jnp.int32) - mx).astype(jnp.float32) / mx
        x_cosine, x_sine = dft_tables(nx, kx_all)
        x_cosine = x_cosine * kx_scaled[:, None]
        x_sine = x_sine * kx_scaled[:, None]
        to_real = jnp.stack([x_sine, -x_cosine], axis=1)
        to_imag = jnp.stack([x_cosine, x_sine], axis=1)
        x_table = jnp.stack([to_real, to_imag], axis=1)
        x_table = x_table.reshape(kx_all * 2, 2, px_size, x_count)
        x_table = jnp.transpose(x_table, (0, 2, 1, 3)).reshape(kx_all * 2, 2 * nx)

        arrived = []
        for part in range(parts):
            low = part * rows
            product = base_flow[:, low : low + rows] * tangent[:, low : low + rows]
            product = product.reshape(x_count * rows, nz)
            z_modes = lax.dot_general(
                z_table, product, (((1,), (1,)), ((), ())), precision=HIGH,
                preferred_element_type=jnp.float32,
            )
            z_modes = z_modes.reshape(px_size, 2 * kz_local, x_count * rows)
            block = lax.all_to_all(z_modes, "px", split_axis=0, concat_axis=0, tiled=True)
            block = block.reshape(px_size, 2, kz_local, x_count, rows)
            block = jnp.transpose(block, (0, 1, 3, 2, 4)).reshape(2 * nx, kz_local * rows)
            forcing = jnp.dot(
                x_table, block, precision=HIGH, preferred_element_type=jnp.float32
            )
            forcing = forcing.reshape(py_size, kx_local * 2, kz_local * rows)
            forcing = lax.all_to_all(forcing, "py", split_axis=0, concat_axis=0, tiled=True)
            arrived.append(forcing.reshape(py_size, kx_local * 2 * kz_local, rows))
        pieces = jnp.stack(arrived, axis=0)
        pieces = jnp.transpose(pieces, (2, 0, 1, 3)).reshape(kx_local * 2 * kz_local, ny)
        left_here = left_basis.reshape(ny, py_size, parts, rows)
        left_here = jnp.transpose(left_here, (0, 2, 1, 3)).reshape(ny, ny)

        projected = lax.dot_general(
            pieces, left_here, (((1,), (1,)), ((), ())), precision=HIGH,
            preferred_element_type=jnp.float32,
        ).reshape(kx_local, 2, kz_local, ny)

        kx_start = lax.axis_index("py") * kx_local
        kz_start = lax.axis_index("px") * kz_local
        columns = kx_start + jnp.arange(kx_local, dtype=jnp.int32)
        kx_here = (columns - mx).astype(jnp.float32) / mx
        kz_here = (kz_start + jnp.arange(kz_local, dtype=jnp.int32) - mz).astype(jnp.float32) / mz
        bounds = lax.dynamic_slice_in_dim(kx_bounds, kz_start, kz_local, 1)
        keep = (columns[:, None] >= bounds[0][None, :]) & (columns[:, None] < bounds[1][None, :])
        shift = kx_here[:, None] ** 2 + kz_here[None, :] ** 2
        gain = 1.0 / (1.0 + eigenvalues[None, None, None, :] + shift[:, None, :, None])
        highest = lax.Precision.HIGHEST
        source_proj = jnp.dot(
            sources, left_basis.T, precision=highest, preferred_element_type=jnp.float32
        )
        wall_map = jnp.dot(
            wall_rows, right_basis, precision=highest, preferred_element_type=jnp.float32
        )
        weighted = jnp.where(keep[:, None, :, None], gain * projected, 0.0)
        wall_values = lax.dot_general(
            wall_map, weighted.reshape(-1, ny), (((1,), (1,)), ((), ())), precision=HIGH,
            preferred_element_type=jnp.float32,
        ).reshape(2, kx_local, 2, kz_local)
        inverse_map = influence.reshape(2, 2, kx_local, 1, kz_local)
        first = -(inverse_map[0, 0] * wall_values[0] + inverse_map[0, 1] * wall_values[1])
        second = -(inverse_map[1, 0] * wall_values[0] + inverse_map[1, 1] * wall_values[1])
        total = weighted + gain * (
            first[..., None] * source_proj[0] + second[..., None] * source_proj[1]
        )
        response = lax.dot_general(
            total.reshape(-1, ny), right_basis, (((1,), (1,)), ((), ())), precision=HIGH,
            preferred_element_type=jnp.float32,
        ).reshape(kx_local, 2, kz_local, ny)
        return jnp.transpose(response, (3, 0, 1, 2))

    return body


def split(value):
    high = value.astype(jnp.bfloat16)
    low = (value - high.astype(jnp.float32)).astype(jnp.bfloat16)
    return high, low


def split_table(value):
    rounded = lax.reduce_precision(value, exponent_bits=8, mantissa_bits=7)
    return rounded.astype(jnp.bfloat16), (value - rounded).astype(jnp.bfloat16)


def dot3(a, b, dims):
    def one(u, v):
        return lax.dot_general(u, v, (dims, ((), ())), preferred_element_type=jnp.float32)

    return one(a[0], b[1]) + one(a[1], b[0]) + one(a[0], b[0])


def z_kernel(groups, high_ref, low_ref, base_ref, tangent_ref, *out_refs):
    step, y_count, nz = base_ref.shape
    product = (base_ref[...] * tangent_ref[...]).reshape(step * y_count, nz)
    modes = dot3((high_ref[...], low_ref[...]), split(product), ((1,), (1,)))
    rows = out_refs[0].shape[0]
    for chunk, out_ref in enumerate(out_refs):
        tiles = out_ref.shape[1]
        flat = out_ref.reshape(rows * tiles * step, LANES)
        for x in range(step):
            pieces = []
            for group in range(groups):
                low = (chunk * groups + group) * rows
                pieces.append(modes[low : low + rows, x * y_count : (x + 1) * y_count])
            whole = jnp.concatenate(pieces, axis=1)
            for tile in range(tiles):
                flat[pl.ds(tile * step + x, rows, stride=tiles * step), :] = whole[
                    :, tile * LANES : (tile + 1) * LANES
                ]


def x_kernel(high_ref, low_ref, data_ref, *out_refs):
    owners, _, parts, tiles, x_count, _ = data_ref.shape
    data = jnp.concatenate(
        [data_ref[:, 0, :, tile].reshape(owners * parts * x_count, LANES) for tile in range(tiles)],
        axis=1,
    )
    forcing = dot3((high_ref[...], low_ref[...]), split(data), ((1,), (0,)))
    rows = out_refs[0].shape[1]
    for ahead, out_ref in enumerate(out_refs):
        out_ref[0] = forcing[ahead * rows : (ahead + 1) * rows]


def wall_kernel(groups, chunks, py_size, *refs):
    data_refs = refs[: chunks * py_size]
    (aux_ref, lane_ref, left_high, left_low, right_high, right_low, out_ref, turned) = refs[
        chunks * py_size :
    ]
    per_chunk, rows, lanes = data_refs[0].shape
    y_count = lanes // groups
    profiles = []
    for chunk in range(chunks):
        for q in range(per_chunk):
            parts = [ref[q] for ref in data_refs[chunk * py_size : (chunk + 1) * py_size]]
            for group in range(groups):
                cut = slice(group * y_count, (group + 1) * y_count)
                profiles.append(jnp.concatenate([part[:, cut] for part in parts], axis=1))
    profiles = jnp.concatenate(profiles, axis=0)
    projected = dot3(
        split(profiles), (left_high[...], left_low[...]), ((1,), (1,))
    )
    aux = aux_ref[...]
    gain = 1.0 / (1.0 + lane_ref[0:1, :] + aux[:, 0:1])
    weighted = jnp.where(aux[:, 1:2] > 0.5, gain * projected, 0.0)
    wall_0 = jnp.sum(weighted * lane_ref[1:2, :], axis=1, keepdims=True)
    wall_1 = jnp.sum(weighted * lane_ref[2:3, :], axis=1, keepdims=True)
    first = -(aux[:, 2:3] * wall_0 + aux[:, 3:4] * wall_1)
    second = -(aux[:, 4:5] * wall_0 + aux[:, 5:6] * wall_1)
    total = weighted + gain * (first * lane_ref[3:4, :] + second * lane_ref[4:5, :])
    response = dot3(split(total), (right_high[...], right_low[...]), ((1,), (1,)))
    kz_count = chunks * per_chunk * groups
    for tile in range(turned.shape[0]):
        cut = slice(tile * LANES, (tile + 1) * LANES)
        for kz in range(kz_count):
            turned[tile, pl.ds(kz, rows, stride=kz_count), :] = response[
                kz * rows : (kz + 1) * rows, cut
            ]
        out_ref[:, :, cut] = turned[tile].reshape(rows, kz_count, LANES)


def make_kernel_body(px_size, py_size, groups):
    def body(
        base_flow,
        tangent,
        kx_bounds,
        left_basis,
        right_basis,
        eigenvalues,
        wall_rows,
        sources,
        influence,
    ):
        x_count, y_count, nz = base_flow.shape
        nx = x_count * px_size
        ny = y_count * py_size
        kz_local = influence.shape[2]
        kx_local = influence.shape[1]
        kz_all = kz_local * px_size
        kx_all = kx_local * py_size
        mx = kx_all // 2
        mz = kz_all // 2
        quarter = kz_local // groups
        chunks = CHUNKS if quarter % CHUNKS == 0 else 1
        per_chunk = quarter // chunks
        lanes = groups * y_count
        tiles = lanes // LANES
        params = pltpu.CompilerParams(vmem_limit_bytes=VMEM_BYTES)

        z_cosine, z_sine = dft_tables(nz, kz_all)
        z_table = jnp.stack([z_cosine, -z_sine], axis=1)
        z_table = z_table.reshape(px_size, chunks, per_chunk, groups, 2, nz)
        z_table = jnp.transpose(z_table, (1, 3, 0, 2, 4, 5)).reshape(2 * kz_all, nz)
        z_high, z_low = split_table(z_table)

        kx_scaled = (jnp.arange(kx_all, dtype=jnp.int32) - mx).astype(jnp.float32) / mx
        x_cosine, x_sine = dft_tables(nx, kx_all)
        x_cosine = x_cosine * kx_scaled[:, None]
        x_sine = x_sine * kx_scaled[:, None]
        to_real = jnp.stack([x_sine, -x_cosine], axis=1)
        to_imag = jnp.stack([x_cosine, x_sine], axis=1)
        x_table = jnp.stack([to_real, to_imag], axis=1)
        x_table = x_table.reshape(kx_all * 2, 2, px_size, x_count)
        x_table = jnp.transpose(x_table, (0, 2, 1, 3)).reshape(kx_all * 2, 2 * nx)
        here = lax.axis_index("py")
        order = (here + jnp.arange(py_size, dtype=jnp.int32)) % py_size
        x_table = jnp.take(x_table.reshape(py_size, 2 * kx_local, 2 * nx), order, axis=0)
        x_table = x_table.reshape(kx_all * 2, 2 * nx)
        x_high, x_low = split_table(x_table)

        step = 8
        rows = px_size * per_chunk * 2
        full = pl.BlockSpec(z_table.shape, lambda i: (0, 0))
        grid_block = pl.BlockSpec((step, y_count, nz), lambda i: (i, 0, 0))
        z_modes = pl.pallas_call(
            lambda *refs: z_kernel(groups, *refs),
            grid=(x_count // step,),
            in_specs=[full, full, grid_block, grid_block],
            out_specs=[pl.BlockSpec((rows, tiles, step, LANES), lambda i: (0, 0, i, 0))] * chunks,
            out_shape=[jax.ShapeDtypeStruct((rows, tiles, x_count, LANES), jnp.float32)] * chunks,
            compiler_params=params,
            cost_estimate=pl.CostEstimate(
                flops=6 * 2 * kz_all * x_count * y_count * nz,
                bytes_accessed=4 * (2 * x_count * y_count * nz + 2 * kz_all * x_count * y_count),
                transcendentals=0,
            ),
            name="z_modes",
        )(z_high, z_low, base_flow, tangent)

        arrived = []
        made = []
        for chunk in range(chunks):
            ready = z_modes[chunk]
            if chunk >= 2:
                ready, made[chunk - 2] = lax.optimization_barrier((ready, made[chunk - 2]))
            block = lax.all_to_all(ready, "px", split_axis=0, concat_axis=0, tiled=True)
            block = block.reshape(px_size, per_chunk, 2, tiles, x_count, LANES)
            full = pl.BlockSpec(x_table.shape, lambda i: (0, 0))
            forcing = pl.pallas_call(
                x_kernel,
                grid=(per_chunk,),
                in_specs=[
                    full,
                    full,
                    pl.BlockSpec(
                        (px_size, 1, 2, tiles, x_count, LANES), lambda i: (0, i, 0, 0, 0, 0)
                    ),
                ],
                out_specs=[pl.BlockSpec((1, 2 * kx_local, lanes), lambda i: (i, 0, 0))] * py_size,
                out_shape=[
                    jax.ShapeDtypeStruct((per_chunk, 2 * kx_local, lanes), jnp.float32)
                ]
                * py_size,
                compiler_params=params,
                cost_estimate=pl.CostEstimate(
                    flops=6 * 2 * kx_all * 2 * nx * per_chunk * lanes,
                    bytes_accessed=4 * (2 * nx + 2 * kx_all) * per_chunk * lanes,
                    transcendentals=0,
                ),
                name="x_modes",
            )(x_high, x_low, block)
            made.append(forcing[0])
            arrived.append(forcing[0])
            for ahead in range(1, py_size):
                pairs = [(j, (j + ahead) % py_size) for j in range(py_size)]
                arrived.append(lax.ppermute(forcing[ahead], "py", pairs))

        kx_start = lax.axis_index("py") * kx_local
        kz_start = lax.axis_index("px") * kz_local
        columns = kx_start + jnp.arange(kx_local, dtype=jnp.int32)
        kx_here = (columns - mx).astype(jnp.float32) / mx
        kz_here = (kz_start + jnp.arange(kz_local, dtype=jnp.int32) - mz).astype(jnp.float32) / mz
        bounds = lax.dynamic_slice_in_dim(kx_bounds, kz_start, kz_local, 1)
        keep = (columns[:, None] >= bounds[0][None, :]) & (columns[:, None] < bounds[1][None, :])
        shift = kx_here[:, None] ** 2 + kz_here[None, :] ** 2
        blank = jnp.zeros_like(shift)
        aux = jnp.stack(
            [shift, keep.astype(jnp.float32)] + [influence[i] for i in range(4)] + [blank] * 2, axis=-1
        )
        kx_step = 8
        kx_blocks = kx_local // kx_step
        aux = jnp.transpose(aux.reshape(kx_blocks, kx_step, kz_local, 8), (0, 2, 1, 3))
        aux = jnp.broadcast_to(aux[:, :, :, None], (kx_blocks, kz_local, kx_step, 2, 8))
        aux = aux.reshape(-1, 8)
        highest = lax.Precision.HIGHEST
        source_proj = jnp.dot(
            sources, left_basis.T, precision=highest, preferred_element_type=jnp.float32
        )
        wall_map = jnp.dot(
            wall_rows, right_basis, precision=highest, preferred_element_type=jnp.float32
        )
        lane_rows = jnp.concatenate(
            [eigenvalues[None], wall_map, source_proj, jnp.zeros((3, ny), jnp.float32)], axis=0
        )
        behind = (here - jnp.arange(py_size, dtype=jnp.int32)) % py_size
        left_here = jnp.take(left_basis.reshape(ny, py_size, y_count), behind, axis=1)
        left_here = left_here.reshape(ny, ny)
        left_high, left_low = split_table(left_here)
        right_high, right_low = split_table(right_basis)
        square = pl.BlockSpec((ny, ny), lambda i: (0, 0))
        block_rows = kz_local * kx_step * 2
        response = pl.pallas_call(
            lambda *refs: wall_kernel(groups, chunks, py_size, *refs),
            grid=(kx_blocks,),
            in_specs=[
                pl.BlockSpec((per_chunk, 2 * kx_step, lanes), lambda i: (0, i, 0))
            ]
            * (chunks * py_size)
            + [
                pl.BlockSpec((block_rows, 8), lambda i: (i, 0)),
                pl.BlockSpec((8, ny), lambda i: (0, 0)),
                square,
                square,
                square,
                square,
            ],
            out_specs=pl.BlockSpec((2 * kx_step, kz_local, ny), lambda i: (i, 0, 0)),
            out_shape=jax.ShapeDtypeStruct((2 * kx_local, kz_local, ny), jnp.float32),
            scratch_shapes=[pltpu.VMEM((ny // LANES, block_rows, LANES), jnp.float32)],
            compiler_params=params,
            cost_estimate=pl.CostEstimate(
                flops=12 * 2 * kx_local * kz_local * ny * ny,
                bytes_accessed=4 * 4 * kx_local * kz_local * ny,
                transcendentals=0,
            ),
            name="wall_normal",
        )(*arrived, aux, lane_rows, left_high, left_low, right_high, right_low)
        response = response.reshape(kx_local, 2, kz_local, ny)
        return jnp.transpose(response, (3, 0, 1, 2))

    return body


def lane_groups(y_count):
    return LANES * y_count // math.gcd(LANES, y_count) // y_count


def solution(mesh):
    px_size = mesh.shape["px"]
    py_size = mesh.shape["py"]

    def body(*arrays):
        x_count, y_count, _ = arrays[0].shape
        kx_local, kz_local = arrays[8].shape[1:]
        groups = lane_groups(y_count)
        fits = (
            x_count % 8 == 0
            and y_count % 8 == 0
            and kx_local % 8 == 0
            and kz_local % 8 == 0
            and kz_local % groups == 0
            and y_count * py_size % LANES == 0
        )
        if fits:
            return make_kernel_body(px_size, py_size, groups)(*arrays)
        return make_body(px_size, py_size)(*arrays)

    placed = (
        P("px", "py", None),
        P("px", "py", None),
        P(),
        P(),
        P(),
        P(),
        P(),
        P(),
        P(None, "py", "px"),
    )
    return jax.shard_map(
        body,
        mesh=mesh,
        in_specs=placed,
        out_specs=P(None, "py", None, "px"),
        check_vma=False,
    )
```
